32 devices in a mesh: row: 8 (over y, x, core), col: 4 (over z).
Axes of the slice: x: 2, y: 2, z: 4, core: 2. Of those that a mesh axis runs over, the one named last changes fastest.
Arguments:
- features: bfloat16 [32, 1024, 1024], P(None, 'row', 'col'), may hold values from -45 to 45
- first_kernel: bfloat16 [3, 3, 32, 32], replicated, may hold values from -0.375 to 0.375
- second_kernel: bfloat16 [3, 3, 32, 32], replicated, may hold values from -0.375 to 0.375
- first_gain: float32 [32], replicated, may hold values from 0.5 to 1.5
- first_shift: float32 [32], replicated, may hold values from -3 to 3
- second_gain: float32 [32], replicated, may hold values from 0.5 to 1.5
- second_shift: float32 [32], replicated, may hold values from -3 to 3
Outputs:
- symmetric_map: bfloat16 [32, 1024, 1024], P(None, 'row', 'col')
The draws below stay inside these ranges and needn't reach their ends.
All inputs are finite; a program needn't handle non-finite values.
Results may differ from the reference program's by a relative error of at most 0.0053.
Values may be sent and summed in bfloat16 or wider, within the bound.
A program may use at most 192 MiB of HBM per device.

```python
import jax
import jax.numpy as jnp
from jax import lax

C = 32
DILATION_STEP = 8
TILE = 128
SIDE = 1024


def draw_features(key, part):
    noise_key = jax.random.fold_in(key, 11)
    band_key = jax.random.fold_in(key, 37)
    across_key = jax.random.fold_in(key, 41)
    offset_key = jax.random.fold_in(key, 53)
    lateral_key = jax.random.fold_in(key, 67)
    band_len = max(TILE // 2, 1)
    band_count = SIDE // band_len
    row_pos = jnp.arange(SIDE, dtype=jnp.float32)
    col_pos = jnp.arange(SIDE, dtype=jnp.float32)
    row_scale = jnp.repeat(jnp.exp(jax.random.uniform(band_key, (band_count,), jnp.float32, -2.3, 1.1)), band_len)
    col_scale = jnp.repeat(jnp.exp(jax.random.uniform(across_key, (band_count,), jnp.float32, -1.2, 1.2)), band_len)
    row_offset = jnp.repeat(jax.random.uniform(offset_key, (band_count,), jnp.float32, -3.0, 3.0), band_len)
    col_offset = jnp.repeat(jax.random.uniform(lateral_key, (band_count,), jnp.float32, -1.5, 1.5), band_len)
    base = jax.random.truncated_normal(noise_key, -4.0, 4.0, (C, SIDE, SIDE), jnp.float32)
    trend = 1.0 + 2.0 * (row_pos[:, None] + col_pos[None, :]) / (2.0 * SIDE - 2.0)
    decay = 0.5 + jnp.exp(-jnp.abs(row_pos[:, None] - col_pos[None, :]) / (SIDE / 8.0))
    band_scale = row_scale[:, None] * col_scale[None, :]
    band_shift = row_offset[:, None] + col_offset[None, :]
    value = 0.5 * base * (trend * decay * band_scale)[None] + band_shift[None]
    return jnp.clip(value, -45.0, 45.0).astype(jnp.bfloat16)


def gaussian(rng, shape, scale, bound, held_as=jnp.bfloat16):
    drawn = jax.random.normal(rng, shape, jnp.float32) * scale
    return jnp.minimum(jnp.maximum(drawn, -bound), bound).astype(held_as)


def setup_inputs(seed: int = 0) -> dict:
    streams_of = jax.random.split(jax.random.key(seed), 8)
    features = draw_features(jax.random.fold_in(streams_of[7], 71), 0)
    first_kernel = gaussian(streams_of[1], (3, 3, C, C), (9 * C) ** -0.5, 0.375)
    second_kernel = gaussian(streams_of[2], (3, 3, C, C), (9 * C) ** -0.5, 0.375)
    first_gain = jnp.clip(1.0 + 0.1 * jax.random.normal(streams_of[3], (C,), jnp.float32), 0.5, 1.5)
    first_shift = gaussian(streams_of[4], (C,), 0.3, 3.0, jnp.float32)
    second_gain = jnp.clip(1.0 + 0.1 * jax.random.normal(streams_of[5], (C,), jnp.float32), 0.5, 1.5)
    second_shift = gaussian(streams_of[6], (C,), 0.3, 3.0, jnp.float32)
    return dict(features=features, first_kernel=first_kernel, second_kernel=second_kernel, first_gain=first_gain, first_shift=first_shift, second_gain=second_gain, second_shift=second_shift)


epsilon = 1e-05

def dilated(receptive_field, filter_weight):
    block_output = lax.conv_general_dilated(receptive_field[None], filter_weight, (1, 1), ((DILATION_STEP, DILATION_STEP), (DILATION_STEP, DILATION_STEP)), rhs_dilation=(DILATION_STEP, DILATION_STEP), dimension_numbers=('NCHW', 'HWOI', 'NCHW'), preferred_element_type=jnp.float32)
    return block_output[0]

def normalized(hidden, gain, shift):
    centre = lax.optimization_barrier(jnp.mean(hidden, axis=(1, 2)))
    centered = hidden - centre[:, None, None]
    spread = lax.optimization_barrier(jnp.mean(centered * centered, axis=(1, 2)))
    factor = gain.astype(jnp.float32) * lax.rsqrt(spread + epsilon)
    return centered * factor[:, None, None] + shift.astype(jnp.float32)[:, None, None]

def reference(features, first_kernel, second_kernel, first_gain, first_shift, second_gain, second_shift):
    first = dilated(features, first_kernel)
    active = jnp.maximum(normalized(first, first_gain, first_shift), 0.0).astype(jnp.bfloat16)
    second = dilated(active, second_kernel)
    summed = (features.astype(jnp.float32) + normalized(second, second_gain, second_shift)).astype(jnp.bfloat16)
    mirrored = jnp.swapaxes(summed, 1, 2)
    return ((summed.astype(jnp.float32) + mirrored.astype(jnp.float32)) * 0.5).astype(jnp.bfloat16)
```

```python
import jax
import jax.numpy as jnp
from jax import lax
from jax.sharding import PartitionSpec as P

DILATION_STEP = 8


epsilon = 1e-05


def with_halo(cells, sides, width):
    for axis, dim in sides:
        count = lax.axis_size(axis)
        ends = count - 1
        head = lax.slice_in_dim(cells, 0, width, axis=dim)
        tail = lax.slice_in_dim(cells, cells.shape[dim] - width, cells.shape[dim], axis=dim)
        cells = jnp.concatenate(
            [
                lax.ppermute(tail, axis, [(i, (i + 1) % count) for i in range(ends)]),
                cells,
                lax.ppermute(head, axis, [((i + 1) % count, i) for i in range(ends)]),
            ],
            axis=dim,
        )
    return cells


def apply_taps(padded, kernels, output_rows, output_columns):
    members = padded.shape[0]
    channels = kernels.shape[3]
    total = jnp.zeros((members, channels, output_rows, output_columns), jnp.float32)
    for filter_row in range(3):
        for filter_column in range(3):
            piece = padded[
                :,
                :,
                filter_row * DILATION_STEP : filter_row * DILATION_STEP + output_rows,
                filter_column * DILATION_STEP : filter_column * DILATION_STEP + output_columns,
            ]
            total = total + jnp.einsum(
                "poc,pchw->pohw",
                kernels[:, filter_row, filter_column],
                piece,
                preferred_element_type=jnp.float32,
            )
    return total


def extend(receptive_field):
    return with_halo(receptive_field, (("row", 2), ("col", 3)), DILATION_STEP)


def channel_affine(inner, gain, total_cells):
    cells = inner.shape[1] * inner.shape[2]
    local = jnp.sum(inner, axis=(1, 2)) / cells
    deviation = inner - local[:, None, None]
    squares = jnp.sum(deviation * deviation, axis=(1, 2))
    gathered = lax.all_gather(jnp.stack([local, squares]), ("row", "col"))
    centre = jnp.mean(gathered[:, 0], axis=0)
    offset = gathered[:, 0] - centre
    spread = jnp.sum(gathered[:, 1] + cells * offset * offset, axis=0) / total_cells
    factor = gain * lax.rsqrt(spread + epsilon)
    return (centre, factor)


def apply_norm(hidden, centre, factor, shift):
    return (hidden - centre[:, None, None]) * factor[:, None, None] + shift[:, None, None]


def residual_block(
    stacked, first_stack, second_stack, first_gain, first_shift, second_gain, second_shift
):
    tile_rows = stacked.shape[2]
    tile_cols = stacked.shape[3]
    row_devs = lax.axis_size("row")
    col_devs = lax.axis_size("col")
    total_cells = float(tile_rows * tile_cols * row_devs * col_devs)
    first = apply_taps(extend(stacked), first_stack, tile_rows, tile_cols)
    centre, factor = channel_affine(first[0], first_gain, total_cells)
    active = jnp.maximum(apply_norm(first, centre, factor, first_shift), 0.0).astype(jnp.bfloat16)
    second = apply_taps(extend(active), second_stack, tile_rows, tile_cols)
    centre_two, factor_two = channel_affine(second[0], second_gain, total_cells)
    return (
        stacked.astype(jnp.float32) + apply_norm(second, centre_two, factor_two, second_shift)
    ).astype(jnp.bfloat16)


def mirror(block):
    row_devs = lax.axis_size("row")
    col_devs = lax.axis_size("col")
    channels, tile_rows, tile_cols = block.shape
    ratio = row_devs // col_devs
    row = lax.axis_index("row")
    arranged = jnp.zeros((channels, tile_rows, tile_cols), block.dtype)
    for step in range(ratio):
        half = (step + row) % ratio
        part = lax.dynamic_slice_in_dim(block, half * tile_rows, tile_rows, axis=2)
        pairs = [
            (r * col_devs + c, (ratio * c + (step + r) % ratio) * col_devs + r // ratio)
            for r in range(row_devs)
            for c in range(col_devs)
        ]
        moved = jnp.swapaxes(lax.ppermute(part, ("row", "col"), pairs), 1, 2)
        place = (row - step) % ratio
        arranged = lax.dynamic_update_slice_in_dim(arranged, moved, place * tile_rows, axis=2)
    return arranged


def per_device(
    features, first_kernel, second_kernel, first_gain, first_shift, second_gain, second_shift
):
    summed = residual_block(
        features[None],
        first_kernel[None],
        second_kernel[None],
        first_gain,
        first_shift,
        second_gain,
        second_shift,
    )[0]
    total = summed.astype(jnp.float32) + mirror(summed).astype(jnp.float32)
    return (total * 0.5).astype(jnp.bfloat16)


def solution(mesh):
    placed = (P(None, "row", "col"), P(), P(), P(), P(), P(), P())
    return jax.shard_map(
        per_device, mesh=mesh, in_specs=placed, out_specs=P(None, "row", "col"), check_vma=False
    )
```

```python
import functools

import jax
import jax.numpy as jnp
from jax import lax
from jax.experimental import pallas as pl
from jax.experimental.pallas import tpu as pltpu
from jax.sharding import PartitionSpec as P

STEP = 8
GROUP = 4
EPSILON = 1e-05
LANES = 128
MESH = pl.DeviceIdType.MESH


def iota(dim):
    return lax.broadcasted_iota(jnp.int32, (LANES, LANES), dim)


def one_hot(mask):
    return jnp.where(mask, 1.0, 0.0).astype(jnp.bfloat16)


def dot(a, b):
    return jnp.dot(a, b, preferred_element_type=jnp.float32)


def block_kernel(
    rows,
    cols,
    x_ref,
    first_ref,
    second_ref,
    scales_ref,
    out_ref,
    pad_one,
    pad_two,
    hidden,
    packed,
    strips,
    col_stats,
    row_stats,
    row_send,
    row_recv,
    col_send,
    col_recv,
    cs_send,
    cs_recv,
    rs_send,
    rs_recv,
):
    row = lax.axis_index("row")
    col = lax.axis_index("col")
    phases, depth, width = x_ref.shape
    chans = scales_ref.shape[1]
    count = depth // chans
    full = depth + 2 * chans
    cells = float(phases * count * width)
    centre = pl.ds(LANES, width)

    barrier = pltpu.get_barrier_semaphore()
    for d in range(1, cols):
        pl.semaphore_signal(
            barrier, inc=1, device_id=(row, lax.rem(col + d, cols)), device_id_type=MESH
        )
    for d in range(1, rows):
        pl.semaphore_signal(
            barrier, inc=1, device_id=(lax.rem(row + d, rows), col), device_id_type=MESH
        )
    pl.semaphore_wait(barrier, rows + cols - 2)

    def row_copy(pad, n, down):
        source = depth if down else chans
        target = 0 if down else depth + chans
        device = jnp.minimum(row + 1, rows - 1) if down else jnp.maximum(row - 1, 0)
        slot = 2 * n + int(down)
        return pltpu.make_async_remote_copy(
            src_ref=pad.at[:, pl.ds(source, chans), centre],
            dst_ref=pad.at[:, pl.ds(target, chans), centre],
            send_sem=row_send.at[slot],
            recv_sem=row_recv.at[slot],
            device_id=(device, col),
            device_id_type=MESH,
        )

    def col_copy(n, right):
        device = jnp.minimum(col + 1, cols - 1) if right else jnp.maximum(col - 1, 0)
        slot = 2 * n + int(right)
        return pltpu.make_async_remote_copy(
            src_ref=packed.at[n],
            dst_ref=strips.at[slot],
            send_sem=col_send.at[slot],
            recv_sem=col_recv.at[slot],
            device_id=(row, device),
            device_id_type=MESH,
        )

    def halo(pad, n):
        up, down = row_copy(pad, n, False), row_copy(pad, n, True)
        left, right = col_copy(n, False), col_copy(n, True)
        has_up, has_down = row > 0, row < rows - 1
        has_left, has_right = col > 0, col < cols - 1

        @pl.when(has_up)
        def _():
            up.start()

        @pl.when(has_down)
        def _():
            down.start()

        blank = jnp.zeros((phases, chans, width), jnp.bfloat16)

        @pl.when(jnp.logical_not(has_up))
        def _():
            pad[:, pl.ds(0, chans), centre] = blank

        @pl.when(jnp.logical_not(has_down))
        def _():
            pad[:, pl.ds(depth + chans, chans), centre] = blank

        @pl.when(jnp.logical_not(has_left))
        def _():
            strips[2 * n + 1] = jnp.zeros((full, LANES), jnp.bfloat16)

        @pl.when(jnp.logical_not(has_right))
        def _():
            strips[2 * n] = jnp.zeros((full, LANES), jnp.bfloat16)

        @pl.when(has_up)
        def _():
            down.wait_recv()
            up.wait_send()

        @pl.when(has_down)
        def _():
            up.wait_recv()
            down.wait_send()

        total = jnp.zeros((full, LANES), jnp.float32)
        i, j = iota(0), iota(1)
        edge = LANES - STEP
        for phase in range(phases):
            at = phase * STEP
            tail = one_hot((i >= edge) & (j == i - edge + at))
            head = one_hot((i < STEP) & (j == i + LANES // 2 + at))
            total += dot(pad[phase, :, pl.ds(width, LANES)], tail)
            total += dot(pad[phase, :, pl.ds(LANES, LANES)], head)
        packed[n] = total.astype(jnp.bfloat16)

        @pl.when(has_left)
        def _():
            left.start()

        @pl.when(has_right)
        def _():
            right.start()

        @pl.when(has_left)
        def _():
            right.wait_recv()
            left.wait_send()

        @pl.when(has_right)
        def _():
            left.wait_recv()
            right.wait_send()

        for phase in range(phases):
            at = phase * STEP
            tail = one_hot((j >= edge) & (i == j - edge + at))
            head = one_hot((j < STEP) & (i == j + LANES // 2 + at))
            pad[phase, :, pl.ds(0, LANES)] = dot(strips[2 * n + 1], tail).astype(jnp.bfloat16)
            pad[phase, :, pl.ds(width + LANES, LANES)] = dot(strips[2 * n], head).astype(
                jnp.bfloat16
            )

    def fold(values):
        total = jnp.sum(values.reshape(-1, chans, width), axis=0)
        return sum(total[:, k : k + LANES] for k in range(0, width, LANES))

    def conv(pad, weights):
        def body(phase, acc):
            shifted = [
                pad[phase, :, pl.ds(LANES + (b - 1) * STEP, width)] for b in range(3)
            ]
            for g in range(count // GROUP):
                low = g * GROUP * chans
                high = low + (GROUP + 2) * chans
                stacked = jnp.concatenate([s[low:high] for s in shifted], axis=0)
                part = dot(weights[...], stacked)
                hidden[phase, pl.ds(low, GROUP * chans), :] = part
                acc = acc + fold(part)
            return acc

        return lax.fori_loop(0, phases, body, jnp.zeros((chans, LANES), jnp.float32))

    def merge(own, other, size, stats, send, recv, n, axis_size, along_row):
        base = n * axis_size
        stats[base, pl.ds(0, chans), :] = own
        stats[base, pl.ds(chans, chans), :] = other
        copies = []
        for d in range(1, axis_size):
            device = (
                (lax.rem(row + d, axis_size), col)
                if along_row
                else (row, lax.rem(col + d, axis_size))
            )
            copy = pltpu.make_async_remote_copy(
                src_ref=stats.at[base],
                dst_ref=stats.at[base + d],
                send_sem=send.at[base + d],
                recv_sem=recv.at[base + d],
                device_id=device,
                device_id_type=MESH,
            )
            copy.start()
            copies.append(copy)
        for copy in copies:
            copy.wait()
        means = [stats[base + d, pl.ds(0, chans), :] for d in range(axis_size)]
        mean = sum(means) / axis_size
        squares = sum(stats[base + d, pl.ds(chans, chans), :] for d in range(axis_size))
        spread = sum((m - mean) * (m - mean) for m in means)
        return mean, squares + size * spread

    def norm(acc, n):
        own = jnp.broadcast_to(jnp.sum(acc, axis=1, keepdims=True) / cells, (chans, LANES))
        wide = jnp.concatenate([own] * (width // LANES), axis=1)

        def body(phase, squares):
            for q in range(count):
                diff = hidden[phase, pl.ds(q * chans, chans), :] - wide
                squares = squares + fold(diff * diff)
            return squares

        squares = lax.fori_loop(0, phases, body, jnp.zeros((chans, LANES), jnp.float32))
        squares = jnp.broadcast_to(jnp.sum(squares, axis=1, keepdims=True), (chans, LANES))
        mean, squares = merge(
            own, squares, cells, col_stats, cs_send, cs_recv, n, cols, False
        )
        mean, squares = merge(
            mean, squares, cells * cols, row_stats, rs_send, rs_recv, n, rows, True
        )
        factor = scales_ref[2 * n] * lax.rsqrt(squares / (cells * (rows * cols)) + EPSILON)
        shift = scales_ref[2 * n + 1]
        repeat = lambda v: jnp.concatenate([v] * (width // LANES), axis=1)
        return repeat(mean), repeat(factor), repeat(shift)

    pad_one[:, pl.ds(chans, depth), centre] = x_ref[...]
    halo(pad_one, 0)
    mean, factor, shift = norm(conv(pad_one, first_ref), 0)

    def activate(phase, carry):
        for q in range(count):
            cell = hidden[phase, pl.ds(q * chans, chans), :]
            cell = jnp.maximum((cell - mean) * factor + shift, 0.0)
            pad_two[phase, pl.ds((q + 1) * chans, chans), centre] = cell.astype(jnp.bfloat16)
        return carry

    lax.fori_loop(0, phases, activate, 0)
    halo(pad_two, 1)
    mean, factor, shift = norm(conv(pad_two, second_ref), 1)

    def finish(phase, carry):
        for q in range(count):
            at = pl.ds(q * chans, chans)
            cell = (hidden[phase, at, :] - mean) * factor + shift
            out_ref[phase, at, :] = (x_ref[phase, at, :].astype(jnp.float32) + cell).astype(
                jnp.bfloat16
            )
        return carry

    lax.fori_loop(0, phases, finish, 0)


def banded(kernel):
    taps = jnp.transpose(kernel, (2, 1, 0, 3))
    rows = [
        jnp.pad(taps, ((0, 0), (0, 0), (q, GROUP - 1 - q), (0, 0))) for q in range(GROUP)
    ]
    return jnp.stack(rows).reshape(GROUP * kernel.shape[2], -1)


def residual_block(rows, cols, features, first, second, scales):
    chans, height, width = features.shape
    count = height // STEP
    depth = count * chans
    x = jnp.transpose(features.reshape(chans, count, STEP, width), (2, 1, 0, 3))
    x = x.reshape(STEP, depth, width)
    full = depth + 2 * chans
    scales = jnp.broadcast_to(jnp.stack(scales)[:, :, None], (4, chans, LANES))
    vmem = pl.BlockSpec(memory_space=pltpu.VMEM)
    dma = pltpu.SemaphoreType.DMA
    summed = pl.pallas_call(
        functools.partial(block_kernel, rows, cols),
        out_shape=jax.ShapeDtypeStruct(x.shape, jnp.bfloat16),
        in_specs=[vmem] * 4,
        out_specs=vmem,
        scratch_shapes=[
            pltpu.VMEM((STEP, full, width + 2 * LANES), jnp.bfloat16),
            pltpu.VMEM((STEP, full, width + 2 * LANES), jnp.bfloat16),
            pltpu.VMEM((STEP, depth, width), jnp.float32),
            pltpu.VMEM((2, full, LANES), jnp.bfloat16),
            pltpu.VMEM((4, full, LANES), jnp.bfloat16),
            pltpu.VMEM((2 * cols, 2 * chans, LANES), jnp.float32),
            pltpu.VMEM((2 * rows, 2 * chans, LANES), jnp.float32),
            dma((4,)),
            dma((4,)),
            dma((4,)),
            dma((4,)),
            dma((2 * cols,)),
            dma((2 * cols,)),
            dma((2 * rows,)),
            dma((2 * rows,)),
        ],
        compiler_params=pltpu.CompilerParams(
            collective_id=0, has_side_effects=True, vmem_limit_bytes=48 * 1024 * 1024
        ),
    )(x, banded(first), banded(second), scales)
    summed = summed.reshape(STEP, count, chans, width)
    return jnp.transpose(summed, (2, 1, 0, 3)).reshape(features.shape)


def mirror(block):
    row_devs = lax.axis_size("row")
    col_devs = lax.axis_size("col")
    channels, tile_rows, tile_cols = block.shape
    ratio = row_devs // col_devs
    row = lax.axis_index("row")
    arranged = jnp.zeros((channels, tile_rows, tile_cols), block.dtype)
    for step in range(ratio):
        half = (step + row) % ratio
        part = lax.dynamic_slice_in_dim(block, half * tile_rows, tile_rows, axis=2)
        pairs = [
            (r * col_devs + c, (ratio * c + (step + r) % ratio) * col_devs + r // ratio)
            for r in range(row_devs)
            for c in range(col_devs)
        ]
        moved = jnp.swapaxes(lax.ppermute(part, ("row", "col"), pairs), 1, 2)
        place = (row - step) % ratio
        arranged = lax.dynamic_update_slice_in_dim(arranged, moved, place * tile_rows, axis=2)
    return arranged


def solution(mesh):
    rows, cols = mesh.shape["row"], mesh.shape["col"]

    def per_device(features, first, second, gain_one, shift_one, gain_two, shift_two):
        scales = (gain_one, shift_one, gain_two, shift_two)
        summed = residual_block(rows, cols, features, first, second, scales)
        total = summed.astype(jnp.float32) + mirror(summed).astype(jnp.float32)
        return (total * 0.5).astype(jnp.bfloat16)

    placed = (P(None, "row", "col"), P(), P(), P(), P(), P(), P())
    return jax.shard_map(
        per_device, mesh=mesh, in_specs=placed, out_specs=P(None, "row", "col"), check_vma=False
    )
```

```python
import functools

import jax
import jax.numpy as jnp
from jax import lax
from jax.experimental import pallas as pl
from jax.experimental.pallas import tpu as pltpu
from jax.sharding import PartitionSpec as P

STEP = 8
GROUP = 4
EPSILON = 1e-05
LANES = 128
MESH = pl.DeviceIdType.MESH


def iota(dim):
    return lax.broadcasted_iota(jnp.int32, (LANES, LANES), dim)


def one_hot(mask):
    return jnp.where(mask, 1.0, 0.0).astype(jnp.bfloat16)


def dot(a, b):
    return jnp.dot(a, b, preferred_element_type=jnp.float32)


def block_kernel(
    rows,
    cols,
    x_ref,
    first_ref,
    second_ref,
    scales_ref,
    out_ref,
    pad_one,
    pad_two,
    hidden,
    packed,
    strips,
    col_stats,
    row_stats,
    row_send,
    row_recv,
    col_send,
    col_recv,
    cs_send,
    cs_recv,
    rs_send,
    rs_recv,
):
    row = lax.axis_index("row")
    col = lax.axis_index("col")
    phases, depth, width = x_ref.shape
    chans = scales_ref.shape[1]
    count = depth // chans
    full = depth + 2 * chans
    cells = float(phases * count * width)
    centre = pl.ds(LANES, width)

    barrier = pltpu.get_barrier_semaphore()
    for d in range(1, cols):
        pl.semaphore_signal(
            barrier, inc=1, device_id=(row, lax.rem(col + d, cols)), device_id_type=MESH
        )
    for d in range(1, rows):
        pl.semaphore_signal(
            barrier, inc=1, device_id=(lax.rem(row + d, rows), col), device_id_type=MESH
        )
    pl.semaphore_wait(barrier, rows + cols - 2)

    def row_copy(pad, n, down):
        source = depth if down else chans
        target = 0 if down else depth + chans
        device = jnp.minimum(row + 1, rows - 1) if down else jnp.maximum(row - 1, 0)
        slot = 2 * n + int(down)
        return pltpu.make_async_remote_copy(
            src_ref=pad.at[:, pl.ds(source, chans), centre],
            dst_ref=pad.at[:, pl.ds(target, chans), centre],
            send_sem=row_send.at[slot],
            recv_sem=row_recv.at[slot],
            device_id=(device, col),
            device_id_type=MESH,
        )

    def col_copy(n, right):
        device = jnp.minimum(col + 1, cols - 1) if right else jnp.maximum(col - 1, 0)
        slot = 2 * n + int(right)
        return pltpu.make_async_remote_copy(
            src_ref=packed.at[n],
            dst_ref=strips.at[slot],
            send_sem=col_send.at[slot],
            recv_sem=col_recv.at[slot],
            device_id=(row, device),
            device_id_type=MESH,
        )

    def halo(pad, n):
        up, down = row_copy(pad, n, False), row_copy(pad, n, True)
        left, right = col_copy(n, False), col_copy(n, True)
        has_up, has_down = row > 0, row < rows - 1
        has_left, has_right = col > 0, col < cols - 1

        @pl.when(has_up)
        def _():
            up.start()

        @pl.when(has_down)
        def _():
            down.start()

        blank = jnp.zeros((phases, chans, width), jnp.bfloat16)

        @pl.when(jnp.logical_not(has_up))
        def _():
            pad[:, pl.ds(0, chans), centre] = blank

        @pl.when(jnp.logical_not(has_down))
        def _():
            pad[:, pl.ds(depth + chans, chans), centre] = blank

        @pl.when(jnp.logical_not(has_left))
        def _():
            strips[2 * n + 1] = jnp.zeros((full, LANES), jnp.bfloat16)

        @pl.when(jnp.logical_not(has_right))
        def _():
            strips[2 * n] = jnp.zeros((full, LANES), jnp.bfloat16)

        @pl.when(has_up)
        def _():
            down.wait_recv()
            up.wait_send()

        @pl.when(has_down)
        def _():
            up.wait_recv()
            down.wait_send()

        total = jnp.zeros((full, LANES), jnp.float32)
        i, j = iota(0), iota(1)
        edge = LANES - STEP
        for phase in range(phases):
            at = phase * STEP
            tail = one_hot((i >= edge) & (j == i - edge + at))
            head = one_hot((i < STEP) & (j == i + LANES // 2 + at))
            total += dot(pad[phase, :, pl.ds(width, LANES)], tail)
            total += dot(pad[phase, :, pl.ds(LANES, LANES)], head)
        packed[n] = total.astype(jnp.bfloat16)

        @pl.when(has_left)
        def _():
            left.start()

        @pl.when(has_right)
        def _():
            right.start()

        @pl.when(has_left)
        def _():
            right.wait_recv()
            left.wait_send()

        @pl.when(has_right)
        def _():
            left.wait_recv()
            right.wait_send()

        for phase in range(phases):
            at = phase * STEP
            tail = one_hot((j >= edge) & (i == j - edge + at))
            head = one_hot((j < STEP) & (i == j + LANES // 2 + at))
            pad[phase, :, pl.ds(0, LANES)] = dot(strips[2 * n + 1], tail).astype(jnp.bfloat16)
            pad[phase, :, pl.ds(width + LANES, LANES)] = dot(strips[2 * n], head).astype(
                jnp.bfloat16
            )

    def fold(values):
        total = jnp.sum(values.reshape(-1, chans, width), axis=0)
        return sum(total[:, k : k + LANES] for k in range(0, width, LANES))

    def conv(pad, weights):
        def body(phase, acc):
            shifted = [
                pad[phase, :, pl.ds(LANES + (b - 1) * STEP, width)] for b in range(3)
            ]
            for g in range(count // GROUP):
                low = g * GROUP * chans
                high = low + (GROUP + 2) * chans
                stacked = jnp.concatenate([s[low:high] for s in shifted], axis=0)
                part = dot(weights[...], stacked)
                hidden[phase, pl.ds(low, GROUP * chans), :] = part
                acc = acc + fold(part)
            return acc

        return lax.fori_loop(0, phases, body, jnp.zeros((chans, LANES), jnp.float32))

    def merge(own, other, size, stats, send, recv, n, axis_size, along_row):
        base = n * axis_size
        stats[base, pl.ds(0, chans), :] = own
        stats[base, pl.ds(chans, chans), :] = other
        copies = []
        for d in range(1, axis_size):
            device = (
                (lax.rem(row + d, axis_size), col)
                if along_row
                else (row, lax.rem(col + d, axis_size))
            )
            copy = pltpu.make_async_remote_copy(
                src_ref=stats.at[base],
                dst_ref=stats.at[base + d],
                send_sem=send.at[base + d],
                recv_sem=recv.at[base + d],
                device_id=device,
                device_id_type=MESH,
            )
            copy.start()
            copies.append(copy)
        for copy in copies:
            copy.wait()
        means = [stats[base + d, pl.ds(0, chans), :] for d in range(axis_size)]
        mean = sum(means) / axis_size
        squares = sum(stats[base + d, pl.ds(chans, chans), :] for d in range(axis_size))
        spread = sum((m - mean) * (m - mean) for m in means)
        return mean, squares + size * spread

    def norm(acc, n):
        own = jnp.broadcast_to(jnp.sum(acc, axis=1, keepdims=True) / cells, (chans, LANES))
        wide = jnp.concatenate([own] * (width // LANES), axis=1)

        def body(phase, squares):
            for q in range(count):
                diff = hidden[phase, pl.ds(q * chans, chans), :] - wide
                squares = squares + fold(diff * diff)
            return squares

        squares = lax.fori_loop(0, phases, body, jnp.zeros((chans, LANES), jnp.float32))
        squares = jnp.broadcast_to(jnp.sum(squares, axis=1, keepdims=True), (chans, LANES))
        mean, squares = merge(
            own, squares, cells, col_stats, cs_send, cs_recv, n, cols, False
        )
        mean, squares = merge(
            mean, squares, cells * cols, row_stats, rs_send, rs_recv, n, rows, True
        )
        factor = scales_ref[2 * n] * lax.rsqrt(squares / (cells * (rows * cols)) + EPSILON)
        shift = scales_ref[2 * n + 1]
        repeat = lambda v: jnp.concatenate([v] * (width // LANES), axis=1)
        return repeat(mean), repeat(factor), repeat(shift)

    pad_one[:, pl.ds(chans, depth), centre] = x_ref[...]
    halo(pad_one, 0)
    mean, factor, shift = norm(conv(pad_one, first_ref), 0)

    def activate(phase, carry):
        for q in range(count):
            cell = hidden[phase, pl.ds(q * chans, chans), :]
            cell = jnp.maximum((cell - mean) * factor + shift, 0.0)
            pad_two[phase, pl.ds((q + 1) * chans, chans), centre] = cell.astype(jnp.bfloat16)
        return carry

    lax.fori_loop(0, phases, activate, 0)
    halo(pad_two, 1)
    mean, factor, shift = norm(conv(pad_two, second_ref), 1)

    def finish(phase, carry):
        for q in range(count):
            at = pl.ds(q * chans, chans)
            cell = (hidden[phase, at, :] - mean) * factor + shift
            out_ref[phase, at, :] = (x_ref[phase, at, :].astype(jnp.float32) + cell).astype(
                jnp.bfloat16
            )
        return carry

    lax.fori_loop(0, phases, finish, 0)


def banded(kernel):
    taps = jnp.transpose(kernel, (2, 1, 0, 3))
    rows = [
        jnp.pad(taps, ((0, 0), (0, 0), (q, GROUP - 1 - q), (0, 0))) for q in range(GROUP)
    ]
    return jnp.stack(rows).reshape(GROUP * kernel.shape[2], -1)


def residual_block(rows, cols, features, first, second, scales):
    chans, height, width = features.shape
    count = height // STEP
    depth = count * chans
    x = jnp.transpose(features.reshape(chans, count, STEP, width), (2, 1, 0, 3))
    x = x.reshape(STEP, depth, width)
    full = depth + 2 * chans
    scales = jnp.broadcast_to(jnp.stack(scales)[:, :, None], (4, chans, LANES))
    vmem = pl.BlockSpec(memory_space=pltpu.VMEM)
    dma = pltpu.SemaphoreType.DMA
    summed = pl.pallas_call(
        functools.partial(block_kernel, rows, cols),
        out_shape=jax.ShapeDtypeStruct(x.shape, jnp.bfloat16),
        in_specs=[vmem] * 4,
        out_specs=vmem,
        scratch_shapes=[
            pltpu.VMEM((STEP, full, width + 2 * LANES), jnp.bfloat16),
            pltpu.VMEM((STEP, full, width + 2 * LANES), jnp.bfloat16),
            pltpu.VMEM((STEP, depth, width), jnp.float32),
            pltpu.VMEM((2, full, LANES), jnp.bfloat16),
            pltpu.VMEM((4, full, LANES), jnp.bfloat16),
            pltpu.VMEM((2 * cols, 2 * chans, LANES), jnp.float32),
            pltpu.VMEM((2 * rows, 2 * chans, LANES), jnp.float32),
            dma((4,)),
            dma((4,)),
            dma((4,)),
            dma((4,)),
            dma((2 * cols,)),
            dma((2 * cols,)),
            dma((2 * rows,)),
            dma((2 * rows,)),
        ],
        compiler_params=pltpu.CompilerParams(
            collective_id=0, has_side_effects=True, vmem_limit_bytes=48 * 1024 * 1024
        ),
    )(x, banded(first), banded(second), scales)
    summed = summed.reshape(STEP, count, chans, width)
    return jnp.transpose(summed, (2, 1, 0, 3)).reshape(features.shape)


def mirror_kernel(
    rows, cols, chunks, s_ref, out_ref, got, relay, send, recv, relay_send, relay_recv
):
    row = lax.axis_index("row")
    col = lax.axis_index("col")
    ratio = rows // cols
    chans, height, _ = s_ref.shape
    pieces = len(chunks)
    block = lax.div(row, ratio)
    part = lax.rem(row, ratio)
    relays = block == col

    barrier = pltpu.get_barrier_semaphore()
    for d in range(1, cols):
        pl.semaphore_signal(
            barrier, inc=1, device_id=(row, lax.rem(col + d, cols)), device_id_type=MESH
        )
    for d in range(1, rows):
        pl.semaphore_signal(
            barrier, inc=1, device_id=(lax.rem(row + d, rows), col), device_id_type=MESH
        )
    for h in range(ratio):

        @pl.when(jnp.logical_not(relays))
        def _(h=h):
            pl.semaphore_signal(
                barrier, inc=1, device_id=(ratio * col + h, block), device_id_type=MESH
            )

    pl.semaphore_wait(barrier, rows + cols - 2 + jnp.where(relays, 0, ratio))

    def span(k):
        low, size, _ = chunks[k]
        return pl.ds(low, size)

    def source(h, k):
        return s_ref.at[span(k), :, pl.ds(h * height, height)]

    def straight(h, k):
        return pltpu.make_async_remote_copy(
            src_ref=source(h, k),
            dst_ref=got.at[part, span(k)],
            send_sem=send.at[h * pieces + k],
            recv_sem=recv.at[part * pieces + k],
            device_id=(ratio * col + h, block),
            device_id_type=MESH,
        )

    def arrive(j, k):
        return pltpu.make_async_remote_copy(
            src_ref=got.at[j, span(k)],
            dst_ref=got.at[j, span(k)],
            send_sem=send.at[j * pieces + k],
            recv_sem=recv.at[j * pieces + k],
            device_id=(row, col),
            device_id_type=MESH,
        )

    def first_leg(h, k, via):
        if via == "col":
            slot = (lax.rem(col - block + cols, cols) - 1) * ratio + h
            device = (row, block)
        else:
            slot = (lax.rem(block - col + cols, cols) - 1) * ratio + part
            device = (ratio * col + h, col)
        return pltpu.make_async_remote_copy(
            src_ref=source(h, k),
            dst_ref=relay.at[slot, span(k)],
            send_sem=send.at[h * pieces + k],
            recv_sem=relay_recv.at[slot * pieces + k],
            device_id=device,
            device_id_type=MESH,
        )

    def second_leg(d, e, k, via):
        slot = (d - 1) * ratio + e
        other = lax.rem(col + d, cols)
        if via == "col":
            device = (ratio * other + e, col)
            target = part
        else:
            device = (row, other)
            target = e
        return pltpu.make_async_remote_copy(
            src_ref=relay.at[slot, span(k)],
            dst_ref=got.at[target, span(k)],
            send_sem=relay_send.at[slot * pieces + k],
            recv_sem=recv.at[target * pieces + k],
            device_id=device,
            device_id_type=MESH,
        )

    @pl.when(jnp.logical_not(relays))
    def _():
        for k in range(pieces):
            for h in range(ratio):
                via = chunks[k][2]
                (first_leg(h, k, via) if via else straight(h, k)).start()

    @pl.when(relays)
    def _():
        for h in range(ratio):

            @pl.when(part != h)
            def _(h=h):
                for k in range(pieces):
                    straight(h, k).start()

            @pl.when(part == h)
            def _(h=h):
                got[h] = s_ref[:, :, h * height : (h + 1) * height]

        for k in range(pieces):
            via = chunks[k][2]
            if via:
                for d in range(1, cols):
                    for e in range(ratio):
                        leg = second_leg(d, e, k, via)
                        slot = (d - 1) * ratio + e
                        pltpu.make_async_remote_copy(
                            src_ref=relay.at[slot, span(k)],
                            dst_ref=relay.at[slot, span(k)],
                            send_sem=relay_send.at[slot * pieces + k],
                            recv_sem=relay_recv.at[slot * pieces + k],
                            device_id=(row, col),
                            device_id_type=MESH,
                        ).wait_recv()
                        leg.start()

    order = [k for k in range(pieces) if not chunks[k][2]]
    order += [k for k in range(pieces) if chunks[k][2]]
    for k in order:
        for j in range(ratio):

            @pl.when(jnp.logical_not(relays & (part == j)))
            def _(j=j, k=k):
                arrive(j, k).wait_recv()

            low, size, _ = chunks[k]
            at = pl.ds(j * height, height)

            def body(c, carry, j=j, at=at):
                turned = jnp.swapaxes(got[j, c].astype(jnp.float32), 0, 1)
                total = s_ref[c, :, at].astype(jnp.float32) + turned
                out_ref[c, :, at] = (total * 0.5).astype(jnp.bfloat16)
                return carry

            lax.fori_loop(low, low + size, body, 0)

    for k in range(pieces):
        for h in range(ratio):

            @pl.when(jnp.logical_not(relays & (part == h)))
            def _(h=h, k=k):
                straight(h, k).wait_send()

    @pl.when(relays)
    def _():
        for k in range(pieces):
            via = chunks[k][2]
            if via:
                for d in range(1, cols):
                    for e in range(ratio):
                        second_leg(d, e, k, via).wait_send()


CHUNKS = ((16, 4, "row"), (20, 4, "row"), (24, 4, "row"), (28, 4, "row"), (0, 8, ""), (8, 8, ""))


def symmetrize(rows, cols, summed):
    chans, height, width = summed.shape
    ratio = rows // cols
    pieces = len(CHUNKS)
    slots = (cols - 1) * ratio
    vmem = pl.BlockSpec(memory_space=pltpu.VMEM)
    dma = pltpu.SemaphoreType.DMA
    return pl.pallas_call(
        functools.partial(mirror_kernel, rows, cols, CHUNKS),
        out_shape=jax.ShapeDtypeStruct(summed.shape, jnp.bfloat16),
        in_specs=[vmem],
        out_specs=vmem,
        scratch_shapes=[
            pltpu.VMEM((ratio, chans, height, height), jnp.bfloat16),
            pltpu.VMEM((slots, chans, height, height), jnp.bfloat16),
            dma((ratio * pieces,)),
            dma((ratio * pieces,)),
            dma((slots * pieces,)),
            dma((slots * pieces,)),
        ],
        compiler_params=pltpu.CompilerParams(
            collective_id=1, has_side_effects=True, vmem_limit_bytes=48 * 1024 * 1024
        ),
    )(summed)


def solution(mesh):
    rows, cols = mesh.shape["row"], mesh.shape["col"]

    def per_device(features, first, second, gain_one, shift_one, gain_two, shift_two):
        scales = (gain_one, shift_one, gain_two, shift_two)
        summed = residual_block(rows, cols, features, first, second, scales)
        return symmetrize(rows, cols, summed)

    placed = (P(None, "row", "col"), P(), P(), P(), P(), P(), P())
    return jax.shard_map(
        per_device, mesh=mesh, in_specs=placed, out_specs=P(None, "row", "col"), check_vma=False
    )
```

```python
import functools

import jax
import jax.numpy as jnp
from jax import lax
from jax.experimental import pallas as pl
from jax.experimental.pallas import tpu as pltpu
from jax.sharding import PartitionSpec as P

STEP = 8
GROUP = 4
EPSILON = 1e-05
LANES = 128
MESH = pl.DeviceIdType.MESH


def iota(dim):
    return lax.broadcasted_iota(jnp.int32, (LANES, LANES), dim)


def one_hot(mask):
    return jnp.where(mask, 1.0, 0.0).astype(jnp.bfloat16)


def dot(a, b):
    return jnp.dot(a, b, preferred_element_type=jnp.float32)


def block_kernel(
    rows,
    cols,
    x_ref,
    first_ref,
    second_ref,
    scales_ref,
    out_ref,
    pad_one,
    pad_two,
    hidden,
    packed,
    strips,
    col_stats,
    row_stats,
    row_send,
    row_recv,
    col_send,
    col_recv,
    cs_send,
    cs_recv,
    rs_send,
    rs_recv,
):
    row = lax.axis_index("row")
    col = lax.axis_index("col")
    phases, depth, width = x_ref.shape
    chans = scales_ref.shape[1]
    count = depth // chans
    full = depth + 2 * chans
    cells = float(phases * count * width)
    centre = pl.ds(LANES, width)

    barrier = pltpu.get_barrier_semaphore()
    for d in range(1, cols):
        pl.semaphore_signal(
            barrier, inc=1, device_id=(row, lax.rem(col + d, cols)), device_id_type=MESH
        )
    for d in range(1, rows):
        pl.semaphore_signal(
            barrier, inc=1, device_id=(lax.rem(row + d, rows), col), device_id_type=MESH
        )
    pl.semaphore_wait(barrier, rows + cols - 2)

    def row_copy(pad, n, down):
        source = depth if down else chans
        target = 0 if down else depth + chans
        device = jnp.minimum(row + 1, rows - 1) if down else jnp.maximum(row - 1, 0)
        slot = 2 * n + int(down)
        return pltpu.make_async_remote_copy(
            src_ref=pad.at[:, pl.ds(source, chans), centre],
            dst_ref=pad.at[:, pl.ds(target, chans), centre],
            send_sem=row_send.at[slot],
            recv_sem=row_recv.at[slot],
            device_id=(device, col),
            device_id_type=MESH,
        )

    def col_copy(n, right):
        device = jnp.minimum(col + 1, cols - 1) if right else jnp.maximum(col - 1, 0)
        slot = 2 * n + int(right)
        return pltpu.make_async_remote_copy(
            src_ref=packed.at[n],
            dst_ref=strips.at[slot],
            send_sem=col_send.at[slot],
            recv_sem=col_recv.at[slot],
            device_id=(row, device),
            device_id_type=MESH,
        )

    def halo(pad, n):
        up, down = row_copy(pad, n, False), row_copy(pad, n, True)
        left, right = col_copy(n, False), col_copy(n, True)
        has_up, has_down = row > 0, row < rows - 1
        has_left, has_right = col > 0, col < cols - 1

        @pl.when(has_up)
        def _():
            up.start()

        @pl.when(has_down)
        def _():
            down.start()

        blank = jnp.zeros((phases, chans, width), jnp.bfloat16)

        @pl.when(jnp.logical_not(has_up))
        def _():
            pad[:, pl.ds(0, chans), centre] = blank

        @pl.when(jnp.logical_not(has_down))
        def _():
            pad[:, pl.ds(depth + chans, chans), centre] = blank

        @pl.when(jnp.logical_not(has_left))
        def _():
            strips[2 * n + 1] = jnp.zeros((full, LANES), jnp.bfloat16)

        @pl.when(jnp.logical_not(has_right))
        def _():
            strips[2 * n] = jnp.zeros((full, LANES), jnp.bfloat16)

        @pl.when(has_up)
        def _():
            down.wait_recv()
            up.wait_send()

        @pl.when(has_down)
        def _():
            up.wait_recv()
            down.wait_send()

        total = jnp.zeros((full, LANES), jnp.float32)
        i, j = iota(0), iota(1)
        edge = LANES - STEP
        for phase in range(phases):
            at = phase * STEP
            tail = one_hot((i >= edge) & (j == i - edge + at))
            head = one_hot((i < STEP) & (j == i + LANES // 2 + at))
            total += dot(pad[phase, :, pl.ds(width, LANES)], tail)
            total += dot(pad[phase, :, pl.ds(LANES, LANES)], head)
        packed[n] = total.astype(jnp.bfloat16)

        @pl.when(has_left)
        def _():
            left.start()

        @pl.when(has_right)
        def _():
            right.start()

        @pl.when(has_left)
        def _():
            right.wait_recv()
            left.wait_send()

        @pl.when(has_right)
        def _():
            left.wait_recv()
            right.wait_send()

        for phase in range(phases):
            at = phase * STEP
            tail = one_hot((j >= edge) & (i == j - edge + at))
            head = one_hot((j < STEP) & (i == j + LANES // 2 + at))
            pad[phase, :, pl.ds(0, LANES)] = dot(strips[2 * n + 1], tail).astype(jnp.bfloat16)
            pad[phase, :, pl.ds(width + LANES, LANES)] = dot(strips[2 * n], head).astype(
                jnp.bfloat16
            )

    def fold(values):
        total = jnp.sum(values.reshape(-1, chans, width), axis=0)
        return sum(total[:, k : k + LANES] for k in range(0, width, LANES))

    def conv(pad, weights):
        def body(phase, acc):
            shifted = [
                pad[phase, :, pl.ds(LANES + (b - 1) * STEP, width)] for b in range(3)
            ]
            for g in range(count // GROUP):
                low = g * GROUP * chans
                high = low + (GROUP + 2) * chans
                stacked = jnp.concatenate([s[low:high] for s in shifted], axis=0)
                part = dot(weights[...], stacked)
                hidden[phase, pl.ds(low, GROUP * chans), :] = part
                acc = acc + fold(part)
            return acc

        return lax.fori_loop(0, phases, body, jnp.zeros((chans, LANES), jnp.float32))

    def merge(own, other, size, stats, send, recv, n, axis_size, along_row):
        base = n * axis_size
        stats[base, pl.ds(0, chans), :] = own
        stats[base, pl.ds(chans, chans), :] = other
        copies = []
        for d in range(1, axis_size):
            device = (
                (lax.rem(row + d, axis_size), col)
                if along_row
                else (row, lax.rem(col + d, axis_size))
            )
            copy = pltpu.make_async_remote_copy(
                src_ref=stats.at[base],
                dst_ref=stats.at[base + d],
                send_sem=send.at[base + d],
                recv_sem=recv.at[base + d],
                device_id=device,
                device_id_type=MESH,
            )
            copy.start()
            copies.append(copy)
        for copy in copies:
            copy.wait()
        means = [stats[base + d, pl.ds(0, chans), :] for d in range(axis_size)]
        mean = sum(means) / axis_size
        squares = sum(stats[base + d, pl.ds(chans, chans), :] for d in range(axis_size))
        spread = sum((m - mean) * (m - mean) for m in means)
        return mean, squares + size * spread

    def norm(acc, n):
        own = jnp.broadcast_to(jnp.sum(acc, axis=1, keepdims=True) / cells, (chans, LANES))
        wide = jnp.concatenate([own] * (width // LANES), axis=1)

        def body(phase, squares):
            for q in range(count):
                diff = hidden[phase, pl.ds(q * chans, chans), :] - wide
                squares = squares + fold(diff * diff)
            return squares

        squares = lax.fori_loop(0, phases, body, jnp.zeros((chans, LANES), jnp.float32))
        squares = jnp.broadcast_to(jnp.sum(squares, axis=1, keepdims=True), (chans, LANES))
        mean, squares = merge(
            own, squares, cells, col_stats, cs_send, cs_recv, n, cols, False
        )
        mean, squares = merge(
            mean, squares, cells * cols, row_stats, rs_send, rs_recv, n, rows, True
        )
        factor = scales_ref[2 * n] * lax.rsqrt(squares / (cells * (rows * cols)) + EPSILON)
        shift = scales_ref[2 * n + 1]
        repeat = lambda v: jnp.concatenate([v] * (width // LANES), axis=1)
        return repeat(mean), repeat(factor), repeat(shift)

    pad_one[:, pl.ds(chans, depth), centre] = x_ref[...]
    halo(pad_one, 0)
    mean, factor, shift = norm(conv(pad_one, first_ref), 0)

    def activate(phase, carry):
        for q in range(count):
            cell = hidden[phase, pl.ds(q * chans, chans), :]
            cell = jnp.maximum((cell - mean) * factor + shift, 0.0)
            pad_two[phase, pl.ds((q + 1) * chans, chans), centre] = cell.astype(jnp.bfloat16)
        return carry

    lax.fori_loop(0, phases, activate, 0)
    halo(pad_two, 1)
    mean, factor, shift = norm(conv(pad_two, second_ref), 1)

    def finish(phase, carry):
        for q in range(count):
            at = pl.ds(q * chans, chans)
            cell = (hidden[phase, at, :] - mean) * factor + shift
            out_ref[phase, at, :] = (x_ref[phase, at, :].astype(jnp.float32) + cell).astype(
                jnp.bfloat16
            )
        return carry

    lax.fori_loop(0, phases, finish, 0)


def banded(kernel):
    taps = jnp.transpose(kernel, (2, 1, 0, 3))
    rows = [
        jnp.pad(taps, ((0, 0), (0, 0), (q, GROUP - 1 - q), (0, 0))) for q in range(GROUP)
    ]
    return jnp.stack(rows).reshape(GROUP * kernel.shape[2], -1)


def residual_block(rows, cols, features, first, second, scales):
    chans, height, width = features.shape
    count = height // STEP
    depth = count * chans
    x = jnp.transpose(features.reshape(chans, count, STEP, width), (2, 1, 0, 3))
    x = x.reshape(STEP, depth, width)
    full = depth + 2 * chans
    scales = jnp.broadcast_to(jnp.stack(scales)[:, :, None], (4, chans, LANES))
    vmem = pl.BlockSpec(memory_space=pltpu.VMEM)
    dma = pltpu.SemaphoreType.DMA
    summed = pl.pallas_call(
        functools.partial(block_kernel, rows, cols),
        out_shape=jax.ShapeDtypeStruct(x.shape, jnp.bfloat16),
        in_specs=[vmem] * 4,
        out_specs=vmem,
        scratch_shapes=[
            pltpu.VMEM((STEP, full, width + 2 * LANES), jnp.bfloat16),
            pltpu.VMEM((STEP, full, width + 2 * LANES), jnp.bfloat16),
            pltpu.VMEM((STEP, depth, width), jnp.float32),
            pltpu.VMEM((2, full, LANES), jnp.bfloat16),
            pltpu.VMEM((4, full, LANES), jnp.bfloat16),
            pltpu.VMEM((2 * cols, 2 * chans, LANES), jnp.float32),
            pltpu.VMEM((2 * rows, 2 * chans, LANES), jnp.float32),
            dma((4,)),
            dma((4,)),
            dma((4,)),
            dma((4,)),
            dma((2 * cols,)),
            dma((2 * cols,)),
            dma((2 * rows,)),
            dma((2 * rows,)),
        ],
        compiler_params=pltpu.CompilerParams(
            collective_id=0, has_side_effects=True, vmem_limit_bytes=48 * 1024 * 1024
        ),
    )(x, banded(first), banded(second), scales)
    summed = summed.reshape(STEP, count, chans, width)
    return jnp.transpose(summed, (2, 1, 0, 3)).reshape(features.shape)


def mirror_kernel(
    rows, cols, chunks, s_ref, out_ref, got, relay, send, recv, relay_send, relay_recv
):
    row = lax.axis_index("row")
    col = lax.axis_index("col")
    ratio = rows // cols
    chans, height, _ = s_ref.shape
    pieces = len(chunks)
    block = lax.div(row, ratio)
    part = lax.rem(row, ratio)
    relays = block == col

    barrier = pltpu.get_barrier_semaphore()
    for d in range(1, cols):
        pl.semaphore_signal(
            barrier, inc=1, device_id=(row, lax.rem(col + d, cols)), device_id_type=MESH
        )
    for d in range(1, rows):
        pl.semaphore_signal(
            barrier, inc=1, device_id=(lax.rem(row + d, rows), col), device_id_type=MESH
        )
    for h in range(ratio):

        @pl.when(jnp.logical_not(relays))
        def _(h=h):
            pl.semaphore_signal(
                barrier, inc=1, device_id=(ratio * col + h, block), device_id_type=MESH
            )

    pl.semaphore_wait(barrier, rows + cols - 2 + jnp.where(relays, 0, ratio))

    def direct(source_col, source_block):
        z, p = lax.rem(source_col, 4), lax.rem(source_block, 4)
        chosen = (z == p) & (lax.rem(source_col + source_block, 8) < 4)
        for a, b in DIRECT:
            chosen = chosen | ((z == a) & (p == b))
        return chosen

    mine = direct(col, block)

    def span(k):
        low, size = chunks[k]
        return pl.ds(low, size)

    def source(h, k):
        return s_ref.at[span(k), :, pl.ds(h * height, height)]

    def straight(h, k):
        return pltpu.make_async_remote_copy(
            src_ref=source(h, k),
            dst_ref=got.at[part, span(k)],
            send_sem=send.at[h * pieces + k],
            recv_sem=recv.at[part * pieces + k],
            device_id=(ratio * col + h, block),
            device_id_type=MESH,
        )

    def arrive(j, k):
        return pltpu.make_async_remote_copy(
            src_ref=got.at[j, span(k)],
            dst_ref=got.at[j, span(k)],
            send_sem=send.at[j * pieces + k],
            recv_sem=recv.at[j * pieces + k],
            device_id=(row, col),
            device_id_type=MESH,
        )

    def first_leg(h, k):
        slot = (lax.rem(block - col + cols, cols) - 1) * ratio + part
        return pltpu.make_async_remote_copy(
            src_ref=source(h, k),
            dst_ref=relay.at[slot, span(k)],
            send_sem=send.at[h * pieces + k],
            recv_sem=relay_recv.at[slot * pieces + k],
            device_id=(ratio * col + h, col),
            device_id_type=MESH,
        )

    def second_leg(d, e, k):
        slot = (d - 1) * ratio + e
        return pltpu.make_async_remote_copy(
            src_ref=relay.at[slot, span(k)],
            dst_ref=got.at[e, span(k)],
            send_sem=relay_send.at[slot * pieces + k],
            recv_sem=recv.at[e * pieces + k],
            device_id=(row, lax.rem(col + d, cols)),
            device_id_type=MESH,
        )

    @pl.when(jnp.logical_not(relays) & mine)
    def _():
        for k in range(pieces):
            for h in range(ratio):
                straight(h, k).start()

    @pl.when(jnp.logical_not(relays | mine))
    def _():
        for k in range(pieces):
            for h in range(ratio):
                first_leg(h, k).start()

    @pl.when(relays)
    def _():
        for h in range(ratio):

            @pl.when(part != h)
            def _(h=h):
                for k in range(pieces):
                    straight(h, k).start()

            @pl.when(part == h)
            def _(h=h):
                got[h] = s_ref[:, :, h * height : (h + 1) * height]

        for k in range(pieces):
            for d in range(1, cols):

                @pl.when(jnp.logical_not(direct(col, lax.rem(col + d, cols))))
                def _(d=d, k=k):
                    for e in range(ratio):
                        slot = (d - 1) * ratio + e
                        pltpu.make_async_remote_copy(
                            src_ref=relay.at[slot, span(k)],
                            dst_ref=relay.at[slot, span(k)],
                            send_sem=relay_send.at[slot * pieces + k],
                            recv_sem=relay_recv.at[slot * pieces + k],
                            device_id=(row, col),
                            device_id_type=MESH,
                        ).wait_recv()
                        second_leg(d, e, k).start()

    for k in range(pieces):
        for j in range(ratio):

            @pl.when(jnp.logical_not(relays & (part == j)))
            def _(j=j, k=k):
                arrive(j, k).wait_recv()

            low, size = chunks[k]
            at = pl.ds(j * height, height)

            def body(c, carry, j=j, at=at):
                turned = jnp.swapaxes(got[j, c].astype(jnp.float32), 0, 1)
                total = s_ref[c, :, at].astype(jnp.float32) + turned
                out_ref[c, :, at] = (total * 0.5).astype(jnp.bfloat16)
                return carry

            lax.fori_loop(low, low + size, body, 0)

    for k in range(pieces):
        for h in range(ratio):

            @pl.when(jnp.logical_not(relays & (part == h)))
            def _(h=h, k=k):
                straight(h, k).wait_send()

    @pl.when(relays)
    def _():
        for k in range(pieces):
            for d in range(1, cols):

                @pl.when(jnp.logical_not(direct(col, lax.rem(col + d, cols))))
                def _(d=d, k=k):
                    for e in range(ratio):
                        second_leg(d, e, k).wait_send()


DIRECT = ((0, 1), (0, 2), (1, 3), (2, 0), (3, 1), (3, 2))


def symmetrize(rows, cols, summed):
    chans, height, width = summed.shape
    ratio = rows // cols
    size = 4 if chans % 4 == 0 else chans
    chunks = tuple((low, size) for low in range(0, chans, size))
    pieces = len(chunks)
    slots = (cols - 1) * ratio
    vmem = pl.BlockSpec(memory_space=pltpu.VMEM)
    dma = pltpu.SemaphoreType.DMA
    return pl.pallas_call(
        functools.partial(mirror_kernel, rows, cols, chunks),
        out_shape=jax.ShapeDtypeStruct(summed.shape, jnp.bfloat16),
        in_specs=[vmem],
        out_specs=vmem,
        scratch_shapes=[
            pltpu.VMEM((ratio, chans, height, height), jnp.bfloat16),
            pltpu.VMEM((slots, chans, height, height), jnp.bfloat16),
            dma((ratio * pieces,)),
            dma((ratio * pieces,)),
            dma((slots * pieces,)),
            dma((slots * pieces,)),
        ],
        compiler_params=pltpu.CompilerParams(
            collective_id=1, has_side_effects=True, vmem_limit_bytes=48 * 1024 * 1024
        ),
    )(summed)


def solution(mesh):
    rows, cols = mesh.shape["row"], mesh.shape["col"]

    def per_device(features, first, second, gain_one, shift_one, gain_two, shift_two):
        scales = (gain_one, shift_one, gain_two, shift_two)
        summed = residual_block(rows, cols, features, first, second, scales)
        return symmetrize(rows, cols, summed)

    placed = (P(None, "row", "col"), P(), P(), P(), P(), P(), P())
    return jax.shard_map(
        per_device, mesh=mesh, in_specs=placed, out_specs=P(None, "row", "col"), check_vma=False
    )
```
